32 devices in a mesh: dom: 8 (over z, y), feat: 4 (over x, core).
Axes of the slice: x: 2, y: 2, z: 4, core: 2. Of those that a mesh axis runs over, the one named last changes fastest.
Arguments:
- features: bfloat16 [65536, 128], P(('dom', 'feat')), may hold values from -6 to 6
- grad_out: bfloat16 [65536, 256], P(('dom', 'feat')), may hold values from -6 to 6
- w_self: bfloat16 [128, 256], replicated, may hold values from -0.5 to 0.5
- w_neigh: bfloat16 [128, 256], replicated, may hold values from -2 to 2
- tile_src: int32 [512, 6], P(('dom', 'feat')), may hold values from 0 to 17, as said below
- tile_vals: int32 [3072, 128, 128], P(('dom', 'feat')), may hold values from 0 to 2
- send_rows: int32 [32, 128], P(('dom', 'feat')), may hold values from -1 to 2047, as said below
- hub_rows: int32 [32, 4], P(('dom', 'feat')), may hold values from 0 to 2047, as said below
Outputs:
- out_nodes: bfloat16 [65536, 256], P(('dom', 'feat'))
- grad_features: float32 [65536, 128], P(('dom', 'feat'))
- grad_w_self: float32 [128, 256], replicated
- grad_w_neigh: float32 [128, 256], replicated
The draws below stay inside these ranges and needn't reach their ends.
Inputs may be any that keep to these rules, and one draw needn't show every extreme that they name: `tile_src`: the first 3 tiles of each row block name column blocks 0 to 15, the other 3 name blocks 16 to 17. `send_rows`: in each device's 4 slots toward one peer the used entries come first; every device fills all 4 slots toward at least one peer and at least one slot toward every peer. `hub_rows`: A device's hub rows are distinct.
All inputs are finite; a program needn't handle non-finite values.
Results may differ from the reference program's by a relative error of at most 0.0054.
Values may be sent and summed in bfloat16 or wider, within the bound.
A program may use at most 64 MiB of HBM per device.

```python
import jax
import jax.numpy as jnp
from jax import lax

F_IN = 128
HID = 256
BLOCK = 128
NODE_DEV = 2048
TILES_LOC = 3
TILES_REM = 3
SLOT = 4
HUB_DEV = 4
TILES = 6
BLOCKS_DEV = 16
HALO = 128
HUBS = 128
SRC_BLOCKS = 18
NODES = 65536
N_DOM = 8
N_FEAT = 4


def draw_tile_src(key, part):
    key = jax.random.fold_in(key, 11)
    key_near, key_far = jax.random.split(key)
    total_rows = N_DOM * N_FEAT * BLOCKS_DEV
    near_ids = jax.random.randint(key_near, (total_rows, TILES_LOC), 0, BLOCKS_DEV)
    far_ids = jax.random.randint(key_far, (total_rows, TILES_REM), BLOCKS_DEV, SRC_BLOCKS)
    return jnp.concatenate([near_ids, far_ids], 1).astype(jnp.int32)


def draw_tile_vals(key, part):
    key = jax.random.fold_in(key, 12)
    key_hit, key_mult = jax.random.split(key)
    shape_all = (N_DOM * N_FEAT * BLOCKS_DEV * TILES, BLOCK, BLOCK)
    is_edge = jax.random.randint(key_hit, shape_all, 0, 64) == 0
    multiple = jax.random.randint(key_mult, shape_all, 1, 3)
    return jnp.where(is_edge, multiple, 0).astype(jnp.int32)


def draw_send_rows(key, part):
    key = jax.random.fold_in(key, 13)
    key_count, key_full, key_rows = jax.random.split(key, 3)
    devices_all = N_DOM * N_FEAT
    counts = jax.random.randint(key_count, (devices_all, devices_all), 1, SLOT + 1)
    full_peer = jax.random.randint(key_full, (devices_all,), 0, devices_all)
    peers = jnp.arange(devices_all, dtype=jnp.int32)
    counts = jnp.where(peers[None, :] == full_peer[:, None], SLOT, counts)
    slot_pos = jnp.arange(SLOT, dtype=jnp.int32)
    is_live = slot_pos[None, None, :] < counts[:, :, None]
    row_ids = jax.random.randint(key_rows, (devices_all, devices_all, SLOT), 0, NODE_DEV)
    return jnp.where(is_live, row_ids, -1).reshape(devices_all, devices_all * SLOT).astype(jnp.int32)


def draw_hub_rows(key, part):
    key = jax.random.fold_in(key, 14)
    key_off, key_low, key_high = jax.random.split(key, 3)
    devices_all = N_DOM * N_FEAT
    stride = NODE_DEV // HUB_DEV
    offsets = jax.random.randint(key_off, (devices_all, HUB_DEV), 0, stride)
    low_dev = jax.random.randint(key_low, (), 0, devices_all)
    high_dev = jax.random.randint(key_high, (), 0, devices_all)
    device_ids = jnp.arange(devices_all, dtype=jnp.int32)[:, None]
    slot_ids = jnp.arange(HUB_DEV, dtype=jnp.int32)[None, :]
    offsets = jnp.where((device_ids == low_dev) & (slot_ids == 0), 0, offsets)
    offsets = jnp.where((device_ids == high_dev) & (slot_ids == HUB_DEV - 1), stride - 1, offsets)
    return (slot_ids * stride + offsets).astype(jnp.int32)


def block_levels(rng, dims, shards, low, largest):
    def one(axis_at, shards_of):
        steps = jax.random.uniform(jax.random.fold_in(jax.random.fold_in(rng, 6), axis_at), (shards_of,), jnp.float32, low / len(shards), largest / len(shards))
        return jnp.repeat(jnp.exp(steps), dims[axis_at] // shards_of).reshape((-1,) + (1,) * (len(dims) - axis_at - 1))

    gain = one(*shards[0])
    for cut in shards[1:]:
        gain = gain * one(*cut)
    return gain


def bell_draw(key, shape, scale, reach, shards=(), held_as=jnp.bfloat16):
    drawn = scale * jax.random.normal(key, shape, jnp.float32)
    if shards:
        drawn = drawn * block_levels(key, shape, shards, -0.22, 0.18)
    return jnp.clip(drawn, -reach, reach).astype(held_as)


def setup_inputs(seed: int = 0) -> dict:
    arg_keys = jax.random.split(jax.random.key(seed), 9)
    return {
        "features": bell_draw(arg_keys[0], (NODES, F_IN), 1.0, 6.0, ((0, 32),)),
        "grad_out": bell_draw(arg_keys[1], (NODES, HID), 1.0, 6.0, ((0, 32),)),
        "w_self": bell_draw(arg_keys[2], (F_IN, HID), F_IN ** -0.5, 0.5),
        "w_neigh": bell_draw(arg_keys[3], (F_IN, HID), (F_IN // 16) ** -0.5, 2.0),
        "tile_src": draw_tile_src(jax.random.fold_in(arg_keys[8], 71), 0),
        "tile_vals": draw_tile_vals(jax.random.fold_in(arg_keys[8], 71), 0),
        "send_rows": draw_send_rows(jax.random.fold_in(arg_keys[8], 71), 0),
        "hub_rows": draw_hub_rows(jax.random.fold_in(arg_keys[8], 71), 0),
    }


def silu_slope(preact):
    sigma = jax.nn.sigmoid(preact)
    return sigma * (1.0 + preact * (1.0 - sigma))


def reference(features, grad_out, w_self, w_neigh, tile_src, tile_vals, send_rows, hub_rows):
    devices_all = N_DOM * N_FEAT
    feat_all = features.reshape(devices_all, NODE_DEV, F_IN)
    grad_all = grad_out.reshape(devices_all, NODE_DEV, HID)
    src_all = tile_src.reshape(devices_all, BLOCKS_DEV, TILES)
    val_all = tile_vals.reshape(devices_all, BLOCKS_DEV, TILES, BLOCK, BLOCK)
    live_all = send_rows >= 0
    safe_all = jnp.maximum(send_rows, 0)
    owners = jnp.arange(devices_all, dtype=jnp.int32)[:, None]
    hub_feat = feat_all[owners, hub_rows].reshape(HUBS, F_IN)

    def one_device(carry, device):
        grad_acc, hub_acc, dws_acc, dwn_acc = carry
        row_ids = lax.dynamic_slice_in_dim(safe_all, device * SLOT, SLOT, 1)
        is_live = lax.dynamic_slice_in_dim(live_all, device * SLOT, SLOT, 1)
        halo_feat = jnp.where(is_live[:, :, None], feat_all[owners, row_ids], jnp.zeros((), jnp.bfloat16))
        halo_feat = halo_feat.reshape(HALO, F_IN)
        own_feat = feat_all[device]
        sources = jnp.concatenate([own_feat, halo_feat, hub_feat], 0).reshape(SRC_BLOCKS, BLOCK, F_IN)
        counts = val_all[device]
        tile_ids = src_all[device]
        degree = jnp.sum(counts, axis=(1, 3)).astype(jnp.float32) + 1.0
        picked = sources[tile_ids]
        summed = jnp.einsum("btij,btjf->bif", counts.astype(jnp.float32), picked.astype(jnp.float32))
        neighbor = (summed / degree[:, :, None]).astype(jnp.bfloat16).reshape(NODE_DEV, F_IN)
        preact = jnp.dot(own_feat, w_self, preferred_element_type=jnp.float32) + jnp.dot(neighbor, w_neigh, preferred_element_type=jnp.float32)
        output = jax.nn.silu(preact).astype(jnp.bfloat16)
        d_pre = (grad_all[device].astype(jnp.float32) * silu_slope(preact)).astype(jnp.bfloat16)
        dws_acc = dws_acc + jnp.dot(own_feat.T, d_pre, preferred_element_type=jnp.float32)
        dwn_acc = dwn_acc + jnp.dot(neighbor.T, d_pre, preferred_element_type=jnp.float32)
        d_neigh = jnp.dot(d_pre, w_neigh.T, preferred_element_type=jnp.float32).reshape(BLOCKS_DEV, BLOCK, F_IN)
        d_neigh = (d_neigh / degree[:, :, None]).astype(jnp.bfloat16)
        pieces = jnp.einsum("btij,bif->btjf", counts.astype(jnp.float32), d_neigh.astype(jnp.float32))
        d_source = jax.ops.segment_sum(pieces.reshape(BLOCKS_DEV * TILES, BLOCK, F_IN), tile_ids.reshape(-1), num_segments=SRC_BLOCKS)
        d_source = d_source.reshape(SRC_BLOCKS * BLOCK, F_IN)
        local_part = jnp.dot(d_pre, w_self.T, preferred_element_type=jnp.float32) + d_source[:NODE_DEV]
        d_halo = d_source[NODE_DEV:NODE_DEV + HALO].astype(jnp.bfloat16)
        d_halo = lax.optimization_barrier(d_halo).astype(jnp.float32).reshape(devices_all, SLOT, F_IN)
        d_halo = jnp.where(is_live[:, :, None], d_halo, jnp.zeros((), jnp.float32))
        grad_acc = grad_acc.at[device].add(local_part)
        grad_acc = grad_acc.at[owners, row_ids].add(d_halo)
        hub_acc = hub_acc + d_source[NODE_DEV + HALO:]
        return (grad_acc, hub_acc, dws_acc, dwn_acc), output

    start = (jnp.zeros((devices_all, NODE_DEV, F_IN), jnp.float32), jnp.zeros((HUBS, F_IN), jnp.float32),
             jnp.zeros((F_IN, HID), jnp.float32), jnp.zeros((F_IN, HID), jnp.float32))
    finals, outputs = lax.scan(one_device, start, jnp.arange(devices_all, dtype=jnp.int32))
    grad_acc, hub_acc, dws_acc, dwn_acc = finals
    grad_acc = grad_acc.at[owners, hub_rows].add(hub_acc.reshape(devices_all, HUB_DEV, F_IN))
    return outputs.reshape(NODES, HID), grad_acc.reshape(NODES, F_IN), dws_acc, dwn_acc
```

```python
import functools

import jax
import jax.numpy as jnp
from jax import lax
from jax.experimental import pallas as pl
from jax.experimental.pallas import tpu as pltpu
from jax.sharding import PartitionSpec as P

MESH = pl.DeviceIdType.MESH
F32 = jnp.float32
BF16 = jnp.bfloat16
VMEM = pl.BlockSpec(memory_space=pltpu.VMEM)


def my_place(n_feat):
    return lax.axis_index("dom") * n_feat + lax.axis_index("feat")


def place_id(q, n_feat):
    return (q // n_feat, lax.rem(q, n_feat))


def greet(n, n_feat):
    me = my_place(n_feat)
    barrier = pltpu.get_barrier_semaphore()

    def signal(d, carry):
        peer = lax.rem(me + d, n)
        pl.semaphore_signal(barrier, inc=1, device_id=place_id(peer, n_feat), device_id_type=MESH)
        return carry

    lax.fori_loop(1, n, signal, 0)
    return barrier


def send_all(n, n_feat, source_of, dest, send_sem, recv_sem):
    me = my_place(n_feat)

    def start(d, carry):
        peer = lax.rem(me + d, n)
        pltpu.make_async_remote_copy(
            src_ref=source_of(peer),
            dst_ref=dest.at[me],
            send_sem=send_sem,
            recv_sem=recv_sem,
            device_id=place_id(peer, n_feat),
            device_id_type=MESH,
        ).start()
        return carry

    lax.fori_loop(1, n, start, 0)


def wait_all(n, ref, sem):
    part = ref.at[pl.ds(0, n - 1)]
    pltpu.make_async_copy(part, part, sem).wait()


def spread_kernel(n, n_feat, ids_ref, feat_ref, recv_ref, send_ref, send_sem, recv_sem):
    barrier = greet(n, n_feat)
    me = my_place(n_feat)
    nodes = feat_ref.shape[0]
    rows = ids_ref.shape[0]
    lanes = lax.broadcasted_iota(jnp.int32, (rows, nodes), 1)
    pick = jnp.where(lanes == ids_ref[...], 1.0, 0.0).astype(BF16)
    picked = jnp.dot(pick, feat_ref[...], preferred_element_type=F32)
    send_ref[...] = picked.reshape(send_ref.shape)
    recv_ref[me] = send_ref[me]
    pl.semaphore_wait(barrier, n - 1)
    send_all(n, n_feat, lambda peer: send_ref.at[peer], recv_ref, send_sem, recv_sem)
    wait_all(n, recv_ref, recv_sem)
    wait_all(n, send_ref, send_sem)


def layer_kernel(
    n, hub_dev, src_ref, vals_ref, feat_ref, far_ref, grad_ref, ws_ref, wn_ref,
    out_ref, gf_ref, back_ref, dw_ref, source_ref, stage_ref, far_acc,
):
    step = pl.program_id(0)
    per_step, tiles, block, _ = vals_ref.shape
    near = tiles // 2
    width = ws_ref.shape[0]
    nodes = feat_ref.shape[0]
    own_blocks = nodes // block
    slots = far_ref.shape[1] - hub_dev
    halo = slots * n

    @pl.when(step == 0)
    def _():
        source_ref[:, width:] = jnp.ones((source_ref.shape[0], width), BF16)
        source_ref[:nodes, :width] = feat_ref[...]
        for p in range(n):
            stage_ref[p * slots : (p + 1) * slots] = far_ref[p, :slots]
            stage_ref[halo + p * hub_dev : halo + (p + 1) * hub_dev] = far_ref[p, slots:]
        source_ref[nodes:, :width] = stage_ref[...].astype(BF16)
        gf_ref[...] = jnp.zeros_like(gf_ref)
        far_acc[...] = jnp.zeros_like(far_acc)
        dw_ref[...] = jnp.zeros_like(dw_ref)

    weights = []
    summed = []
    for i in range(per_step):
        b = step * per_step + i
        wide = jnp.concatenate([vals_ref[i, t].astype(F32).astype(BF16) for t in range(tiles)], 1)
        picked = jnp.concatenate(
            [source_ref[pl.ds(pl.multiple_of(src_ref[b, t] * block, block), block)] for t in range(tiles)], 0
        )
        weights.append(wide)
        summed.append(jnp.dot(wide, picked, preferred_element_type=F32))
    summed = jnp.concatenate(summed, 0)
    inv = 1.0 / (summed[:, width:] + 1.0)
    neighbor = (summed[:, :width] * inv).astype(BF16)
    rows = per_step * block
    first = pl.multiple_of(step * rows, rows)
    own = feat_ref[pl.ds(first, rows)]
    both = jnp.concatenate([own, neighbor], 1)
    w_both = jnp.concatenate([ws_ref[...], wn_ref[...]], 0)
    preact = jnp.dot(both, w_both, preferred_element_type=F32)
    sigma = 0.5 * jnp.tanh(0.5 * preact) + 0.5
    out = preact * sigma
    out_ref[...] = out.astype(BF16)
    slope = sigma + out * (1.0 - sigma)
    d_pre = (grad_ref[...].astype(F32) * slope).astype(BF16)
    dw = lax.dot_general(both, d_pre, (((0,), (0,)), ((), ())), preferred_element_type=F32)
    dw_ref[0] += dw[:, :width]
    dw_ref[1] += dw[:, width:]
    d_both = lax.dot_general(d_pre, w_both, (((1,), (1,)), ((), ())), preferred_element_type=F32)
    gf_ref[pl.ds(first, rows)] += d_both[:, :width]
    d_neigh = (d_both[:, width:] * inv).astype(BF16)
    for i in range(per_step):
        b = step * per_step + i
        pieces = lax.dot_general(
            weights[i], d_neigh[i * block : (i + 1) * block], (((0,), (0,)), ((), ())),
            preferred_element_type=F32,
        )
        for t in range(tiles):
            piece = pieces[t * block : (t + 1) * block]
            if t < near:
                at = pl.ds(pl.multiple_of(src_ref[b, t] * block, block), block)
                gf_ref[at] += piece
            else:
                at = pl.ds(pl.multiple_of((src_ref[b, t] - own_blocks) * block, block), block)
                far_acc[at] += piece

    @pl.when(step == pl.num_programs(0) - 1)
    def _():
        for p in range(n):
            d_halo = far_acc[p * slots : (p + 1) * slots]
            back_ref[p, :slots] = d_halo.astype(BF16).astype(F32)
            back_ref[p, slots:] = far_acc[halo + p * hub_dev : halo + (p + 1) * hub_dev]


def collect_kernel(
    n, n_feat, ids_ref, back_ref, dw_ref, gf_ref, out_gf, out_ws, out_wn,
    recv_ref, part_ref, total_ref, full_ref, send_sem, recv_sem,
):
    barrier = greet(n, n_feat)
    me = my_place(n_feat)
    recv_ref[me] = back_ref[me]
    part_ref[me] = dw_ref[me]
    pl.semaphore_wait(barrier, n - 1)
    send_all(n, n_feat, lambda peer: dw_ref.at[peer], part_ref, send_sem.at[0], recv_sem.at[0])
    send_all(n, n_feat, lambda peer: back_ref.at[peer], recv_ref, send_sem.at[1], recv_sem.at[1])
    wait_all(n, part_ref, recv_sem.at[0])
    total_ref[...] = jnp.sum(part_ref[...], axis=0).astype(total_ref.dtype)
    full_ref[me] = total_ref[...]
    send_all(n, n_feat, lambda peer: total_ref, full_ref, send_sem.at[2], recv_sem.at[2])
    wait_all(n, recv_ref, recv_sem.at[1])
    rows = back_ref.shape[0] * back_ref.shape[1]
    width = back_ref.shape[2]
    nodes = gf_ref.shape[0]
    arrived = recv_ref[...].reshape(rows, width)
    high = arrived.astype(BF16)
    low = (arrived - high.astype(F32)).astype(BF16)
    terms = jnp.concatenate([high, low], 1)
    part = nodes // 4
    for c in range(4):
        at = lax.broadcasted_iota(jnp.int32, (part, rows), 0) + c * part
        place = jnp.where(at == ids_ref[...], 1.0, 0.0).astype(BF16)
        added = jnp.dot(place, terms, preferred_element_type=F32)
        span = pl.ds(c * part, part)
        out_gf[span] = gf_ref[span] + (added[:, :width] + added[:, width:])
    wait_all(n, full_ref, recv_sem.at[2])
    full = full_ref[...].astype(F32).reshape(2, 2, out_ws.shape[0], width)
    for h in range(2):
        out_ws[:, h * width : (h + 1) * width] = full[h, 0]
        out_wn[:, h * width : (h + 1) * width] = full[h, 1]
    wait_all(n, dw_ref, send_sem.at[0])
    wait_all(n, back_ref, send_sem.at[1])
    wait_all(n, full_ref, send_sem.at[2])


def per_device(features, grad_out, w_self, w_neigh, tile_src, tile_vals, send_rows, hub_rows):
    n_dom = lax.axis_size("dom")
    n_feat = lax.axis_size("feat")
    n = n_dom * n_feat
    nodes, width = features.shape
    hidden = w_self.shape[1]
    blocks, tiles = tile_src.shape
    block = tile_vals.shape[1]
    hub_dev = hub_rows.shape[1]
    slots = send_rows.shape[1] // n
    group = slots + hub_dev
    far = n * group
    ids = jnp.concatenate(
        [send_rows.reshape(n, slots), jnp.broadcast_to(hub_rows, (n, hub_dev))], 1
    )
    sems = pltpu.SemaphoreType.DMA

    received = pl.pallas_call(
        functools.partial(spread_kernel, n, n_feat),
        out_shape=jax.ShapeDtypeStruct((n, group, width), F32),
        in_specs=[VMEM, VMEM],
        out_specs=VMEM,
        scratch_shapes=[pltpu.VMEM((n, group, width), F32), sems, sems],
        compiler_params=pltpu.CompilerParams(
            collective_id=0, has_side_effects=True, vmem_limit_bytes=48 << 20
        ),
        name="spread_rows",
    )(ids.reshape(far, 1), features)

    per_step = 4
    steps = blocks // per_step
    rows = per_step * block
    whole = lambda s, ids: (0, 0)
    whole3 = lambda s, ids: (0, 0, 0)
    output, grad_near, back, dw = pl.pallas_call(
        functools.partial(layer_kernel, n, hub_dev),
        grid_spec=pltpu.PrefetchScalarGridSpec(
            num_scalar_prefetch=1,
            grid=(steps,),
            in_specs=[
                pl.BlockSpec((per_step, tiles, block, block), lambda s, ids: (s, 0, 0, 0)),
                pl.BlockSpec((nodes, width), whole),
                pl.BlockSpec((n, group, width), whole3),
                pl.BlockSpec((rows, hidden), lambda s, ids: (s, 0)),
                pl.BlockSpec((width, hidden), whole),
                pl.BlockSpec((width, hidden), whole),
            ],
            out_specs=[
                pl.BlockSpec((rows, hidden), lambda s, ids: (s, 0)),
                pl.BlockSpec((nodes, width), whole),
                pl.BlockSpec((n, group, width), whole3),
                pl.BlockSpec((2, 2 * width, width), whole3),
            ],
            scratch_shapes=[
                pltpu.VMEM((nodes + far, 2 * width), BF16),
                pltpu.VMEM((far, width), F32),
                pltpu.VMEM((far, width), F32),
            ],
        ),
        out_shape=[
            jax.ShapeDtypeStruct((nodes, hidden), BF16),
            jax.ShapeDtypeStruct((nodes, width), F32),
            jax.ShapeDtypeStruct((n, group, width), F32),
            jax.ShapeDtypeStruct((2, 2 * width, width), F32),
        ],
        compiler_params=pltpu.CompilerParams(
            dimension_semantics=("arbitrary",), vmem_limit_bytes=48 << 20
        ),
        name="layer_both_ways",
    )(tile_src, tile_vals.reshape(blocks, tiles, block, block), features, received, grad_out, w_self, w_neigh)

    piece = 4 * width // n
    held = BF16 if piece % 16 == 0 else F32
    grad_feat, grad_ws, grad_wn = pl.pallas_call(
        functools.partial(collect_kernel, n, n_feat),
        out_shape=[
            jax.ShapeDtypeStruct((nodes, width), F32),
            jax.ShapeDtypeStruct((width, hidden), F32),
            jax.ShapeDtypeStruct((width, hidden), F32),
        ],
        in_specs=[VMEM] * 4,
        out_specs=[VMEM] * 3,
        scratch_shapes=[
            pltpu.VMEM((n, group, width), F32),
            pltpu.VMEM((n, piece, width), F32),
            pltpu.VMEM((piece, width), held),
            pltpu.VMEM((n, piece, width), held),
            sems((3,)),
            sems((3,)),
        ],
        compiler_params=pltpu.CompilerParams(
            collective_id=1, has_side_effects=True, vmem_limit_bytes=48 << 20
        ),
        name="collect_gradients",
    )(ids.reshape(1, far), back, dw.reshape(n, piece, width), grad_near)
    return output, grad_feat, grad_ws, grad_wn


def solution(mesh):
    nodes = P(("dom", "feat"), None)
    return jax.shard_map(
        per_device,
        mesh=mesh,
        in_specs=(nodes, nodes, P(), P(), nodes, P(("dom", "feat"), None, None), nodes, nodes),
        out_specs=(nodes, nodes, P(), P()),
        check_vma=False,
    )
```

```python
import functools

import jax
import jax.numpy as jnp
from jax import lax
from jax.experimental import pallas as pl
from jax.experimental.pallas import tpu as pltpu
from jax.sharding import PartitionSpec as P

MESH = pl.DeviceIdType.MESH
F32 = jnp.float32
BF16 = jnp.bfloat16
VMEM = pl.BlockSpec(memory_space=pltpu.VMEM)


def my_place(n_feat):
    return lax.axis_index("dom") * n_feat + lax.axis_index("feat")


def place_id(q, n_feat):
    return (q // n_feat, lax.rem(q, n_feat))


def greet(n, n_feat):
    me = my_place(n_feat)
    barrier = pltpu.get_barrier_semaphore()

    def signal(d, carry):
        peer = lax.rem(me + d, n)
        pl.semaphore_signal(barrier, inc=1, device_id=place_id(peer, n_feat), device_id_type=MESH)
        return carry

    lax.fori_loop(1, n, signal, 0)
    return barrier


def send_all(count, me, place_of, source_of, dest, send_sem, recv_sem):
    def start(d, carry):
        peer = lax.rem(me + d, count)
        pltpu.make_async_remote_copy(
            src_ref=source_of(peer),
            dst_ref=dest.at[me],
            send_sem=send_sem,
            recv_sem=recv_sem,
            device_id=place_of(peer),
            device_id_type=MESH,
        ).start()
        return carry

    lax.fori_loop(1, count, start, 0)


def wait_all(count, ref, sem):
    part = ref.at[pl.ds(0, count - 1)]
    pltpu.make_async_copy(part, part, sem).wait()


def one_hot_rows(ids_ref, first, count):
    at = lax.broadcasted_iota(jnp.int32, (count, ids_ref.shape[1]), 0) + first
    return jnp.where(at == ids_ref[...], 1.0, 0.0).astype(BF16)


OVER_ROWS = (((0,), (0,)), ((), ()))
OVER_COLS = (((1,), (1,)), ((), ()))


def spread_kernel(
    n, n_feat, per_step, send_rows, hub_rows, feat_hbm, grad_hbm, ws_hbm, wn_hbm, vals_hbm,
    source_ref, wide_ref, grad_ref, w_ref,
    feat_ref, vals_ref, stage_ref, send_ref, recv_ref, load_sem, vals_sem, send_sem, recv_sem,
):
    nodes, width = feat_ref.shape
    steps, group, block, _ = vals_ref.shape
    tiles = group // per_step
    halo, hub_dev = send_rows.shape[1], hub_rows.shape[1]
    slots = halo // n
    load_feat = pltpu.make_async_copy(feat_hbm, feat_ref, load_sem.at[0])
    load_feat.start()

    def load_vals(c):
        return pltpu.make_async_copy(vals_hbm.at[c], vals_ref.at[c], vals_sem.at[c])

    for c in range(steps):
        load_vals(c).start()
    loads = [
        pltpu.make_async_copy(grad_hbm, grad_ref, load_sem.at[1]),
        pltpu.make_async_copy(ws_hbm, w_ref.at[:width], load_sem.at[2]),
        pltpu.make_async_copy(wn_hbm, w_ref.at[width:], load_sem.at[3]),
    ]
    for load in loads:
        load.start()
    barrier = greet(n, n_feat)
    me = my_place(n_feat)
    load_feat.wait()
    feat = feat_ref[...]
    picked = lax.dot_general(one_hot_rows(send_rows, 0, nodes), feat, OVER_ROWS, preferred_element_type=F32)
    hubs = lax.dot_general(one_hot_rows(hub_rows, 0, nodes), feat, OVER_ROWS, preferred_element_type=F32)
    for p in range(n):
        send_ref[p, :slots] = picked[p * slots : (p + 1) * slots]
        send_ref[p, slots:] = hubs
    recv_ref[me] = send_ref[me]
    pl.semaphore_wait(barrier, n - 1)
    send_all(n, me, lambda q: place_id(q, n_feat), lambda q: send_ref.at[q], recv_ref, send_sem, recv_sem)
    source_ref[:nodes, :width] = feat
    source_ref[:, width:] = jnp.ones((source_ref.shape[0], width), BF16)

    def convert(c, carry):
        load_vals(c).wait()
        for i in range(per_step):
            b = c * per_step + i
            wide_ref[b] = jnp.concatenate(
                [vals_ref[c, i * tiles + t].astype(F32).astype(BF16) for t in range(tiles)], 1
            )
        return carry

    lax.fori_loop(0, steps, convert, 0)
    for load in loads:
        load.wait()
    wait_all(n, recv_ref, recv_sem)
    for p in range(n):
        stage_ref[p * slots : (p + 1) * slots] = recv_ref[p, :slots]
        stage_ref[halo + p * hub_dev : halo + (p + 1) * hub_dev] = recv_ref[p, slots:]
    source_ref[nodes:, :width] = stage_ref[...].astype(BF16)
    wait_all(n, send_ref, send_sem)


def layer_kernel(
    n, hub_dev, per_step, src_ref, source_ref, wide_ref, grad_ref, w_ref,
    out_hbm, gf_ref, back_ref, dw_ref, out_ref, far_acc, out_sem,
):
    blocks, block, reach = wide_ref.shape
    tiles = reach // block
    near = tiles // 2
    nodes, width = gf_ref.shape
    own_blocks = nodes // block
    slots = back_ref.shape[1] - hub_dev
    halo = slots * n
    gf_ref[...] = jnp.zeros_like(gf_ref)
    far_acc[...] = jnp.zeros_like(far_acc)
    dw_ref[...] = jnp.zeros_like(dw_ref)
    rows = per_step * block

    def flush(step):
        span = pl.ds(pl.multiple_of(step * rows, rows), rows)
        return pltpu.make_async_copy(out_ref.at[span], out_hbm.at[span], out_sem.at[step])

    def body(step, carry):
        summed = []
        for i in range(per_step):
            b = step * per_step + i
            picked = jnp.concatenate(
                [source_ref[pl.ds(pl.multiple_of(src_ref[b, t] * block, block), block)] for t in range(tiles)], 0
            )
            summed.append(jnp.dot(wide_ref[b], picked, preferred_element_type=F32))
        summed = jnp.concatenate(summed, 0)
        inv = 1.0 / (summed[:, width:] + 1.0)
        neighbor = (summed[:, :width] * inv).astype(BF16)
        span = pl.ds(pl.multiple_of(step * rows, rows), rows)
        both = jnp.concatenate([source_ref[span, :width], neighbor], 1)
        preact = jnp.dot(both, w_ref[...], preferred_element_type=F32)
        sigma = 0.5 * jnp.tanh(0.5 * preact) + 0.5
        out = preact * sigma
        out_ref[span] = out.astype(BF16)
        flush(step).start()
        slope = sigma + out * (1.0 - sigma)
        d_pre = (grad_ref[span].astype(F32) * slope).astype(BF16)
        d_both = lax.dot_general(d_pre, w_ref[...], OVER_COLS, preferred_element_type=F32)
        d_neigh = (d_both[:, width:] * inv).astype(BF16)
        gf_ref[span] += d_both[:, :width]
        dw = lax.dot_general(both, d_pre, OVER_ROWS, preferred_element_type=F32)
        dw_ref[0] += dw[:, :width]
        dw_ref[1] += dw[:, width:]
        for i in range(per_step):
            b = step * per_step + i
            pieces = lax.dot_general(
                wide_ref[b], d_neigh[i * block : (i + 1) * block], OVER_ROWS, preferred_element_type=F32
            )
            for t in range(tiles):
                piece = pieces[t * block : (t + 1) * block]
                if t < near:
                    at = pl.ds(pl.multiple_of(src_ref[b, t] * block, block), block)
                    gf_ref[at] += piece
                else:
                    at = pl.ds(pl.multiple_of((src_ref[b, t] - own_blocks) * block, block), block)
                    far_acc[at] += piece
        return carry

    lax.fori_loop(0, blocks // per_step, body, 0)
    for p in range(n):
        d_halo = far_acc[p * slots : (p + 1) * slots]
        back_ref[p, :slots] = d_halo.astype(BF16).astype(F32)
        back_ref[p, slots:] = far_acc[halo + p * hub_dev : halo + (p + 1) * hub_dev]
    for step in range(blocks // per_step):
        flush(step).wait()


def collect_kernel(
    n_dom, n_feat, send_rows, hub_rows, back_ref, dw_ref, gf_ref, out_gf, out_ws, out_wn,
    recv_ref, stage_ref, part_ref, mid_ref, thin_ref, small_ref, line_ref, full_ref, send_sem, recv_sem,
):
    n = n_dom * n_feat
    dom, feat = lax.axis_index("dom"), lax.axis_index("feat")
    barrier = greet(n, n_feat)
    me = my_place(n_feat)
    recv_ref[me] = back_ref[me]
    part_ref[feat] = dw_ref[feat]
    pl.semaphore_wait(barrier, n - 1)
    along = lambda q: (dom, q)
    across = lambda q: (q, feat)
    send_all(n_feat, feat, along, lambda q: dw_ref.at[q], part_ref, send_sem.at[0], recv_sem.at[0])
    send_all(n, me, lambda q: place_id(q, n_feat), lambda q: back_ref.at[q], recv_ref, send_sem.at[1], recv_sem.at[1])
    wait_all(n_feat, part_ref, recv_sem.at[0])
    mid_ref[...] = jnp.sum(part_ref[...], axis=0).reshape(mid_ref.shape)
    thin_ref[dom] = mid_ref[dom]
    send_all(n_dom, dom, across, lambda q: mid_ref.at[q], thin_ref, send_sem.at[2], recv_sem.at[2])

    wait_all(n, recv_ref, recv_sem.at[1])
    slots = back_ref.shape[1] - hub_rows.shape[1]
    width = back_ref.shape[2]
    nodes = gf_ref.shape[0]
    for p in range(n):
        stage_ref[p * slots : (p + 1) * slots] = recv_ref[p, :slots]
    terms = stage_ref[...].astype(BF16)
    hub_sum = jnp.sum(recv_ref[...], axis=0)[slots:]
    hub_high = hub_sum.astype(BF16)
    rest = hub_sum - hub_high.astype(F32)
    hub_mid = rest.astype(BF16)
    hub_low = (rest - hub_mid.astype(F32)).astype(BF16)
    hub_terms = jnp.concatenate([hub_high, hub_mid, hub_low], 1)
    part = nodes // 4

    def scatter(c):
        span = pl.ds(c * part, part)
        added = jnp.dot(one_hot_rows(send_rows, c * part, part), terms, preferred_element_type=F32)
        hubs = jnp.dot(one_hot_rows(hub_rows, c * part, part), hub_terms, preferred_element_type=F32)
        hubs = (hubs[:, :width] + hubs[:, width : 2 * width]) + hubs[:, 2 * width :]
        out_gf[span] = gf_ref[span] + (added + hubs)

    scatter(0)
    wait_all(n_dom, thin_ref, recv_sem.at[2])
    small_ref[...] = jnp.sum(thin_ref[...], axis=0).astype(small_ref.dtype)
    line_ref[dom] = small_ref[...]
    send_all(n_dom, dom, across, lambda q: small_ref, line_ref, send_sem.at[3], recv_sem.at[3])
    scatter(1)
    wait_all(n_dom, line_ref, recv_sem.at[3])
    full_ref[feat] = line_ref[...]
    send_all(n_feat, feat, along, lambda q: line_ref, full_ref, send_sem.at[4], recv_sem.at[4])
    scatter(2)
    scatter(3)
    wait_all(n_feat, full_ref, recv_sem.at[4])
    full = full_ref[...].astype(F32).reshape(2, 2, out_ws.shape[0], width)
    for h in range(2):
        out_ws[:, h * width : (h + 1) * width] = full[h, 0]
        out_wn[:, h * width : (h + 1) * width] = full[h, 1]
    wait_all(n_feat, dw_ref, send_sem.at[0])
    wait_all(n, back_ref, send_sem.at[1])
    wait_all(n_dom, mid_ref, send_sem.at[2])
    wait_all(n_dom, line_ref, send_sem.at[3])
    wait_all(n_feat, full_ref, send_sem.at[4])


def per_device(features, grad_out, w_self, w_neigh, tile_src, tile_vals, send_rows, hub_rows):
    n_dom = lax.axis_size("dom")
    n_feat = lax.axis_size("feat")
    n = n_dom * n_feat
    nodes, width = features.shape
    hidden = w_self.shape[1]
    blocks, tiles = tile_src.shape
    block = tile_vals.shape[1]
    hub_dev = hub_rows.shape[1]
    halo = send_rows.shape[1]
    group = halo // n + hub_dev
    far = n * group
    sems = pltpu.SemaphoreType.DMA
    shape = jax.ShapeDtypeStruct
    anywhere = pl.BlockSpec(memory_space=pl.ANY)
    scalars = pl.BlockSpec(memory_space=pltpu.SMEM)
    per_step = 4
    steps = blocks // per_step
    limit = 32 << 20

    source, wide, grad, w_both = pl.pallas_call(
        functools.partial(spread_kernel, n, n_feat, per_step),
        out_shape=[
            shape((nodes + far, 2 * width), BF16),
            shape((blocks, block, tiles * block), BF16),
            shape((nodes, hidden), BF16),
            shape((2 * width, hidden), BF16),
        ],
        in_specs=[VMEM, VMEM] + [anywhere] * 5,
        out_specs=[VMEM] * 4,
        scratch_shapes=[
            pltpu.VMEM((nodes, width), BF16),
            pltpu.VMEM((steps, per_step * tiles, block, block), jnp.int32),
            pltpu.VMEM((far, width), F32),
            pltpu.VMEM((n, group, width), F32),
            pltpu.VMEM((n, group, width), F32),
            sems((4,)),
            sems((steps,)),
            sems,
            sems,
        ],
        compiler_params=pltpu.CompilerParams(
            collective_id=0, has_side_effects=True, vmem_limit_bytes=limit
        ),
        name="spread_rows",
    )(
        send_rows, hub_rows, features, grad_out, w_self, w_neigh,
        tile_vals.reshape(steps, per_step * tiles, block, block),
    )

    output, grad_near, back, dw = pl.pallas_call(
        functools.partial(layer_kernel, n, hub_dev, per_step),
        out_shape=[
            shape((nodes, hidden), BF16),
            shape((nodes, width), F32),
            shape((n, group, width), F32),
            shape((2, 2 * width, width), F32),
        ],
        in_specs=[scalars] + [VMEM] * 4,
        out_specs=[anywhere] + [VMEM] * 3,
        scratch_shapes=[
            pltpu.VMEM((nodes, hidden), BF16),
            pltpu.VMEM((far, width), F32),
            sems((steps,)),
        ],
        compiler_params=pltpu.CompilerParams(vmem_limit_bytes=limit),
        name="layer_both_ways",
    )(tile_src, source, wide, grad, w_both)

    chunk = 4 * width // n_feat
    piece = chunk // n_dom
    held = BF16 if piece % 16 == 0 else F32
    grad_feat, grad_ws, grad_wn = pl.pallas_call(
        functools.partial(collect_kernel, n_dom, n_feat),
        out_shape=[shape((nodes, width), F32), shape((width, hidden), F32), shape((width, hidden), F32)],
        in_specs=[VMEM] * 5,
        out_specs=[VMEM] * 3,
        scratch_shapes=[
            pltpu.VMEM((n, group, width), F32),
            pltpu.VMEM((halo, width), F32),
            pltpu.VMEM((n_feat, chunk, width), F32),
            pltpu.VMEM((n_dom, piece, width), F32),
            pltpu.VMEM((n_dom, piece, width), F32),
            pltpu.VMEM((piece, width), held),
            pltpu.VMEM((n_dom, piece, width), held),
            pltpu.VMEM((n_feat, n_dom, piece, width), held),
            sems((5,)),
            sems((5,)),
        ],
        compiler_params=pltpu.CompilerParams(
            collective_id=1, has_side_effects=True, vmem_limit_bytes=limit
        ),
        name="collect_gradients",
    )(send_rows, hub_rows, back, dw.reshape(n_feat, chunk, width), grad_near)
    return output, grad_feat, grad_ws, grad_wn


def solution(mesh):
    nodes = P(("dom", "feat"), None)
    return jax.shard_map(
        per_device,
        mesh=mesh,
        in_specs=(nodes, nodes, P(), P(), nodes, P(("dom", "feat"), None, None), nodes, nodes),
        out_specs=(nodes, nodes, P(), P()),
        check_vma=False,
    )
```

```python
import functools

import jax
import jax.numpy as jnp
from jax import lax
from jax.experimental import pallas as pl
from jax.experimental.pallas import tpu as pltpu
from jax.sharding import PartitionSpec as P

MESH = pl.DeviceIdType.MESH
F32 = jnp.float32
BF16 = jnp.bfloat16
VMEM = pl.BlockSpec(memory_space=pltpu.VMEM)


def my_place(n_feat):
    return lax.axis_index("dom") * n_feat + lax.axis_index("feat")


def place_id(q, n_feat):
    return (q // n_feat, lax.rem(q, n_feat))


def greet(n, n_feat):
    me = my_place(n_feat)
    barrier = pltpu.get_barrier_semaphore()

    def signal(d, carry):
        peer = lax.rem(me + d, n)
        pl.semaphore_signal(barrier, inc=1, device_id=place_id(peer, n_feat), device_id_type=MESH)
        return carry

    lax.fori_loop(1, n, signal, 0)
    return barrier


def send_all(count, me, place_of, source_of, dest, send_sem, recv_sem):
    def start(d, carry):
        peer = lax.rem(me + d, count)
        pltpu.make_async_remote_copy(
            src_ref=source_of(peer),
            dst_ref=dest.at[me],
            send_sem=send_sem,
            recv_sem=recv_sem,
            device_id=place_of(peer),
            device_id_type=MESH,
        ).start()
        return carry

    lax.fori_loop(1, count, start, 0)


def wait_all(count, ref, sem):
    part = ref.at[pl.ds(0, count - 1)]
    pltpu.make_async_copy(part, part, sem).wait()


def one_hot_rows(ids_ref, first, count):
    at = lax.broadcasted_iota(jnp.int32, (count, ids_ref.shape[1]), 0) + first
    return jnp.where(at == ids_ref[...], 1.0, 0.0).astype(BF16)


OVER_ROWS = (((0,), (0,)), ((), ()))
OVER_COLS = (((1,), (1,)), ((), ()))


def spread_kernel(
    n, n_feat, per_step, send_rows, hub_rows, feat_hbm, grad_hbm, ws_hbm, wn_hbm, vals_hbm,
    source_ref, wide_ref, grad_ref, w_ref,
    feat_ref, vals_ref, stage_ref, send_ref, recv_ref, load_sem, vals_sem, send_sem, recv_sem,
):
    nodes, width = feat_ref.shape
    steps, group, block, _ = vals_ref.shape
    tiles = group // per_step
    halo, hub_dev = send_rows.shape[1], hub_rows.shape[1]
    slots = halo // n
    load_feat = pltpu.make_async_copy(feat_hbm, feat_ref, load_sem.at[0])
    load_feat.start()

    def load_vals(c):
        return pltpu.make_async_copy(vals_hbm.at[c], vals_ref.at[c], vals_sem.at[c])

    for c in range(steps):
        load_vals(c).start()
    loads = [
        pltpu.make_async_copy(grad_hbm, grad_ref, load_sem.at[1]),
        pltpu.make_async_copy(ws_hbm, w_ref.at[:width], load_sem.at[2]),
        pltpu.make_async_copy(wn_hbm, w_ref.at[width:], load_sem.at[3]),
    ]
    for load in loads:
        load.start()
    barrier = greet(n, n_feat)
    me = my_place(n_feat)
    load_feat.wait()
    feat = feat_ref[...]
    picked = lax.dot_general(one_hot_rows(send_rows, 0, nodes), feat, OVER_ROWS, preferred_element_type=F32)
    hubs = lax.dot_general(one_hot_rows(hub_rows, 0, nodes), feat, OVER_ROWS, preferred_element_type=F32)
    for p in range(n):
        send_ref[p, :slots] = picked[p * slots : (p + 1) * slots]
        send_ref[p, slots:] = hubs
    recv_ref[me] = send_ref[me]
    pl.semaphore_wait(barrier, n - 1)
    send_all(n, me, lambda q: place_id(q, n_feat), lambda q: send_ref.at[q], recv_ref, send_sem, recv_sem)
    source_ref[:nodes, :width] = feat
    source_ref[:, width:] = jnp.ones((source_ref.shape[0], width), BF16)

    def convert(c, carry):
        load_vals(c).wait()
        for i in range(per_step):
            b = c * per_step + i
            wide_ref[b] = jnp.concatenate(
                [vals_ref[c, i * tiles + t].astype(F32).astype(BF16) for t in range(tiles)], 1
            )
        return carry

    lax.fori_loop(0, steps, convert, 0)
    for load in loads:
        load.wait()
    wait_all(n, recv_ref, recv_sem)
    for p in range(n):
        stage_ref[p * slots : (p + 1) * slots] = recv_ref[p, :slots]
        stage_ref[halo + p * hub_dev : halo + (p + 1) * hub_dev] = recv_ref[p, slots:]
    source_ref[nodes:, :width] = stage_ref[...].astype(BF16)
    wait_all(n, send_ref, send_sem)


def layer_kernel(
    n, hub_dev, per_step, src_ref, source_ref, wide_ref, grad_ref, w_ref,
    out_hbm, gf_ref, back_ref, dw_ref, out_ref, far_acc, out_sem,
):
    blocks, block, reach = wide_ref.shape
    tiles = reach // block
    near = tiles // 2
    nodes, width = gf_ref.shape
    own_blocks = nodes // block
    slots = back_ref.shape[1] - hub_dev
    halo = slots * n
    gf_ref[...] = jnp.zeros_like(gf_ref)
    far_acc[...] = jnp.zeros_like(far_acc)
    dw_ref[...] = jnp.zeros_like(dw_ref)
    rows = per_step * block

    def flush(step):
        span = pl.ds(pl.multiple_of(step * rows, rows), rows)
        return pltpu.make_async_copy(out_ref.at[span], out_hbm.at[span], out_sem.at[step])

    def body(step, carry):
        summed = []
        for i in range(per_step):
            b = step * per_step + i
            picked = jnp.concatenate(
                [source_ref[pl.ds(pl.multiple_of(src_ref[t, b] * block, block), block)] for t in range(tiles)], 0
            )
            summed.append(jnp.dot(wide_ref[b], picked, preferred_element_type=F32))
        summed = jnp.concatenate(summed, 0)
        inv = 1.0 / (summed[:, width:] + 1.0)
        neighbor = (summed[:, :width] * inv).astype(BF16)
        span = pl.ds(pl.multiple_of(step * rows, rows), rows)
        both = jnp.concatenate([source_ref[span, :width], neighbor], 1)
        preact = jnp.dot(both, w_ref[...], preferred_element_type=F32)
        sigma = 0.5 * jnp.tanh(0.5 * preact) + 0.5
        out = preact * sigma
        out_ref[span] = out.astype(BF16)
        flush(step).start()
        slope = sigma + out * (1.0 - sigma)
        d_pre = (grad_ref[span].astype(F32) * slope).astype(BF16)
        d_both = lax.dot_general(d_pre, w_ref[...], OVER_COLS, preferred_element_type=F32)
        d_neigh = (d_both[:, width:] * inv).astype(BF16)
        gf_ref[span] += d_both[:, :width]
        dw = lax.dot_general(both, d_pre, OVER_ROWS, preferred_element_type=F32)
        dw_ref[0] += dw[:, :width]
        dw_ref[1] += dw[:, width:]
        for i in range(per_step):
            b = step * per_step + i
            pieces = lax.dot_general(
                wide_ref[b], d_neigh[i * block : (i + 1) * block], OVER_ROWS, preferred_element_type=F32
            )
            for t in range(tiles):
                piece = pieces[t * block : (t + 1) * block]
                if t < near:
                    at = pl.ds(pl.multiple_of(src_ref[t, b] * block, block), block)
                    gf_ref[at] += piece
                else:
                    at = pl.ds(pl.multiple_of((src_ref[t, b] - own_blocks) * block, block), block)
                    far_acc[at] += piece
        return carry

    lax.fori_loop(0, blocks // per_step, body, 0)
    for p in range(n):
        d_halo = far_acc[p * slots : (p + 1) * slots]
        back_ref[p, :slots] = d_halo.astype(BF16).astype(F32)
        back_ref[p, slots:] = far_acc[halo + p * hub_dev : halo + (p + 1) * hub_dev]
    for step in range(blocks // per_step):
        flush(step).wait()


def collect_kernel(
    n_dom, n_feat, send_rows, hub_rows, back_ref, dw_ref, gf_ref, out_gf, out_ws, out_wn,
    recv_ref, stage_ref, part_ref, mid_ref, thin_ref, small_ref, line_ref, full_ref, send_sem, recv_sem,
):
    n = n_dom * n_feat
    dom, feat = lax.axis_index("dom"), lax.axis_index("feat")
    barrier = greet(n, n_feat)
    me = my_place(n_feat)
    recv_ref[me] = back_ref[me]
    part_ref[feat] = dw_ref[feat]
    pl.semaphore_wait(barrier, n - 1)
    along = lambda q: (dom, q)
    across = lambda q: (q, feat)
    send_all(n_feat, feat, along, lambda q: dw_ref.at[q], part_ref, send_sem.at[0], recv_sem.at[0])
    send_all(n, me, lambda q: place_id(q, n_feat), lambda q: back_ref.at[q], recv_ref, send_sem.at[1], recv_sem.at[1])
    wait_all(n_feat, part_ref, recv_sem.at[0])
    mid_ref[...] = jnp.sum(part_ref[...], axis=0).reshape(mid_ref.shape)
    thin_ref[dom] = mid_ref[dom]
    send_all(n_dom, dom, across, lambda q: mid_ref.at[q], thin_ref, send_sem.at[2], recv_sem.at[2])

    wait_all(n, recv_ref, recv_sem.at[1])
    slots = back_ref.shape[1] - hub_rows.shape[1]
    width = back_ref.shape[2]
    nodes = gf_ref.shape[0]
    for p in range(n):
        stage_ref[p * slots : (p + 1) * slots] = recv_ref[p, :slots]
    terms = stage_ref[...].astype(BF16)
    hub_sum = jnp.sum(recv_ref[...], axis=0)[slots:]
    hub_high = hub_sum.astype(BF16)
    rest = hub_sum - hub_high.astype(F32)
    hub_mid = rest.astype(BF16)
    hub_low = (rest - hub_mid.astype(F32)).astype(BF16)
    hub_terms = jnp.concatenate([hub_high, hub_mid, hub_low], 1)
    part = nodes // 4

    def scatter(c):
        span = pl.ds(c * part, part)
        added = jnp.dot(one_hot_rows(send_rows, c * part, part), terms, preferred_element_type=F32)
        hubs = jnp.dot(one_hot_rows(hub_rows, c * part, part), hub_terms, preferred_element_type=F32)
        hubs = (hubs[:, :width] + hubs[:, width : 2 * width]) + hubs[:, 2 * width :]
        out_gf[span] = gf_ref[span] + (added + hubs)

    scatter(0)
    wait_all(n_dom, thin_ref, recv_sem.at[2])
    small_ref[...] = jnp.sum(thin_ref[...], axis=0).astype(small_ref.dtype)
    line_ref[dom] = small_ref[...]
    send_all(n_dom, dom, across, lambda q: small_ref, line_ref, send_sem.at[3], recv_sem.at[3])
    scatter(1)
    wait_all(n_dom, line_ref, recv_sem.at[3])
    full_ref[feat] = line_ref[...]
    send_all(n_feat, feat, along, lambda q: line_ref, full_ref, send_sem.at[4], recv_sem.at[4])
    scatter(2)
    scatter(3)
    wait_all(n_feat, full_ref, recv_sem.at[4])
    full = full_ref[...].astype(F32).reshape(2, 2, out_ws.shape[0], width)
    for h in range(2):
        out_ws[:, h * width : (h + 1) * width] = full[h, 0]
        out_wn[:, h * width : (h + 1) * width] = full[h, 1]
    wait_all(n_feat, dw_ref, send_sem.at[0])
    wait_all(n, back_ref, send_sem.at[1])
    wait_all(n_dom, mid_ref, send_sem.at[2])
    wait_all(n_dom, line_ref, send_sem.at[3])
    wait_all(n_feat, full_ref, send_sem.at[4])


def per_device(features, grad_out, w_self, w_neigh, tile_src, tile_vals, send_rows, hub_rows):
    n_dom = lax.axis_size("dom")
    n_feat = lax.axis_size("feat")
    n = n_dom * n_feat
    nodes, width = features.shape
    hidden = w_self.shape[1]
    blocks, tiles = tile_src.shape
    block = tile_vals.shape[1]
    hub_dev = hub_rows.shape[1]
    halo = send_rows.shape[1]
    group = halo // n + hub_dev
    far = n * group
    sems = pltpu.SemaphoreType.DMA
    shape = jax.ShapeDtypeStruct
    anywhere = pl.BlockSpec(memory_space=pl.ANY)
    scalars = pl.BlockSpec(memory_space=pltpu.SMEM)
    per_step = 4
    steps = blocks // per_step
    limit = 32 << 20

    source, wide, grad, w_both = pl.pallas_call(
        functools.partial(spread_kernel, n, n_feat, per_step),
        out_shape=[
            shape((nodes + far, 2 * width), BF16),
            shape((blocks, block, tiles * block), BF16),
            shape((nodes, hidden), BF16),
            shape((2 * width, hidden), BF16),
        ],
        in_specs=[VMEM, VMEM] + [anywhere] * 5,
        out_specs=[VMEM] * 4,
        scratch_shapes=[
            pltpu.VMEM((nodes, width), BF16),
            pltpu.VMEM((steps, per_step * tiles, block, block), jnp.int32),
            pltpu.VMEM((far, width), F32),
            pltpu.VMEM((n, group, width), F32),
            pltpu.VMEM((n, group, width), F32),
            sems((4,)),
            sems((steps,)),
            sems,
            sems,
        ],
        compiler_params=pltpu.CompilerParams(
            collective_id=0, has_side_effects=True, vmem_limit_bytes=47 << 20
        ),
        name="spread_rows",
    )(
        send_rows, hub_rows, features, grad_out, w_self, w_neigh,
        tile_vals.reshape(steps, per_step * tiles, block, block),
    )

    output, grad_near, back, dw = pl.pallas_call(
        functools.partial(layer_kernel, n, hub_dev, per_step),
        out_shape=[
            shape((nodes, hidden), BF16),
            shape((nodes, width), F32),
            shape((n, group, width), F32),
            shape((2, 2 * width, width), F32),
        ],
        in_specs=[scalars] + [VMEM] * 4,
        out_specs=[anywhere] + [VMEM] * 3,
        scratch_shapes=[
            pltpu.VMEM((nodes, hidden), BF16),
            pltpu.VMEM((far, width), F32),
            sems((steps,)),
        ],
        compiler_params=pltpu.CompilerParams(vmem_limit_bytes=limit),
        name="layer_both_ways",
    )(tile_src.T, source, wide, grad, w_both)

    chunk = 4 * width // n_feat
    piece = chunk // n_dom
    held = BF16 if piece % 16 == 0 else F32
    grad_feat, grad_ws, grad_wn = pl.pallas_call(
        functools.partial(collect_kernel, n_dom, n_feat),
        out_shape=[shape((nodes, width), F32), shape((width, hidden), F32), shape((width, hidden), F32)],
        in_specs=[VMEM] * 5,
        out_specs=[VMEM] * 3,
        scratch_shapes=[
            pltpu.VMEM((n, group, width), F32),
            pltpu.VMEM((halo, width), F32),
            pltpu.VMEM((n_feat, chunk, width), F32),
            pltpu.VMEM((n_dom, piece, width), F32),
            pltpu.VMEM((n_dom, piece, width), F32),
            pltpu.VMEM((piece, width), held),
            pltpu.VMEM((n_dom, piece, width), held),
            pltpu.VMEM((n_feat, n_dom, piece, width), held),
            sems((5,)),
            sems((5,)),
        ],
        compiler_params=pltpu.CompilerParams(
            collective_id=1, has_side_effects=True, vmem_limit_bytes=limit
        ),
        name="collect_gradients",
    )(send_rows, hub_rows, back, dw.reshape(n_feat, chunk, width), grad_near)
    return output, grad_feat, grad_ws, grad_wn


def solution(mesh):
    nodes = P(("dom", "feat"), None)
    return jax.shard_map(
        per_device,
        mesh=mesh,
        in_specs=(nodes, nodes, P(), P(), nodes, P(("dom", "feat"), None, None), nodes, nodes),
        out_specs=(nodes, nodes, P(), P()),
        check_vma=False,
    )
```

```python
import functools

import jax
import jax.numpy as jnp
from jax import lax
from jax.experimental import pallas as pl
from jax.experimental.pallas import tpu as pltpu
from jax.sharding import PartitionSpec as P

MESH = pl.DeviceIdType.MESH
F32 = jnp.float32
BF16 = jnp.bfloat16
VMEM = pl.BlockSpec(memory_space=pltpu.VMEM)


def greet(n_dom, n_feat):
    dom, feat = lax.axis_index("dom"), lax.axis_index("feat")
    barrier = pltpu.get_barrier_semaphore()

    def signal_feat(d, carry):
        pl.semaphore_signal(barrier, inc=1, device_id=(dom, lax.rem(feat + d, n_feat)), device_id_type=MESH)
        return carry

    def signal_dom(d, carry):
        pl.semaphore_signal(barrier, inc=1, device_id=(lax.rem(dom + d, n_dom), feat), device_id_type=MESH)
        return carry

    lax.fori_loop(1, n_feat, signal_feat, 0)
    lax.fori_loop(1, n_dom, signal_dom, 0)
    return barrier


def send_all(count, me, place_of, source_of, dest, send_sem, recv_sem):
    def start(d, carry):
        peer = lax.rem(me + d, count)
        pltpu.make_async_remote_copy(
            src_ref=source_of(peer),
            dst_ref=dest.at[me],
            send_sem=send_sem,
            recv_sem=recv_sem,
            device_id=place_of(peer),
            device_id_type=MESH,
        ).start()
        return carry

    lax.fori_loop(1, count, start, 0)


def wait_all(count, ref, sem):
    part = ref.at[pl.ds(0, count - 1)]
    pltpu.make_async_copy(part, part, sem).wait()


def one_hot_rows(ids_ref, first, count):
    at = lax.broadcasted_iota(jnp.int32, (count, ids_ref.shape[1]), 0) + first
    return jnp.where(at == ids_ref[...], 1.0, 0.0).astype(BF16)


OVER_ROWS = (((0,), (0,)), ((), ()))
OVER_COLS = (((1,), (1,)), ((), ()))


def spread_kernel(
    n_dom, n_feat, per_step, send_rows, hub_rows, feat_hbm, grad_hbm, ws_hbm, wn_hbm, vals_hbm,
    source_ref, wide_ref, grad_ref, w_ref,
    feat_ref, vals_ref, stage_ref, send_ref, hop_ref, recv_ref, load_sem, vals_sem, send_sem, recv_sem,
):
    nodes, width = feat_ref.shape
    steps, group, block, _ = vals_ref.shape
    tiles = group // per_step
    halo, hub_dev = send_rows.shape[1], hub_rows.shape[1]
    n = n_dom * n_feat
    slots = halo // n
    load_feat = pltpu.make_async_copy(feat_hbm, feat_ref, load_sem.at[0])
    load_feat.start()

    def load_vals(c):
        return pltpu.make_async_copy(vals_hbm.at[c], vals_ref.at[c], vals_sem.at[c])

    for c in range(steps):
        load_vals(c).start()
    loads = [
        pltpu.make_async_copy(grad_hbm, grad_ref, load_sem.at[1]),
        pltpu.make_async_copy(ws_hbm, w_ref.at[:width], load_sem.at[2]),
        pltpu.make_async_copy(wn_hbm, w_ref.at[width:], load_sem.at[3]),
    ]
    for load in loads:
        load.start()
    barrier = greet(n_dom, n_feat)
    dom, at_feat = lax.axis_index("dom"), lax.axis_index("feat")
    load_feat.wait()
    feat = feat_ref[...]
    picked = lax.dot_general(one_hot_rows(send_rows, 0, nodes), feat, OVER_ROWS, preferred_element_type=F32)
    hubs = lax.dot_general(one_hot_rows(hub_rows, 0, nodes), feat, OVER_ROWS, preferred_element_type=F32)
    for p in range(n):
        send_ref[p % n_feat, p // n_feat, :slots] = picked[p * slots : (p + 1) * slots]
        send_ref[p % n_feat, p // n_feat, slots:] = hubs
    hop_ref[at_feat] = send_ref[at_feat]
    pl.semaphore_wait(barrier, n_feat + n_dom - 2)
    send_all(n_feat, at_feat, lambda q: (dom, q), lambda q: send_ref.at[q], hop_ref, send_sem.at[0], recv_sem.at[0])
    source_ref[:nodes, :width] = feat
    source_ref[:, width:] = jnp.ones((source_ref.shape[0], width), BF16)

    def convert(c, carry):
        load_vals(c).wait()
        for i in range(per_step):
            b = c * per_step + i
            wide_ref[b] = jnp.concatenate(
                [vals_ref[c, i * tiles + t].astype(F32).astype(BF16) for t in range(tiles)], 1
            )
        return carry

    lax.fori_loop(0, steps // 2, convert, 0)
    wait_all(n_feat, hop_ref, recv_sem.at[0])
    recv_ref[dom] = hop_ref[:, dom]
    send_all(n_dom, dom, lambda q: (q, at_feat), lambda q: hop_ref.at[:, q], recv_ref, send_sem.at[1], recv_sem.at[1])
    lax.fori_loop(steps // 2, steps, convert, 0)
    for load in loads:
        load.wait()
    wait_all(n_dom, recv_ref, recv_sem.at[1])
    for p in range(n):
        stage_ref[p * slots : (p + 1) * slots] = recv_ref[p // n_feat, p % n_feat, :slots]
        stage_ref[halo + p * hub_dev : halo + (p + 1) * hub_dev] = recv_ref[p // n_feat, p % n_feat, slots:]
    source_ref[nodes:, :width] = stage_ref[...].astype(BF16)
    wait_all(n_feat, send_ref, send_sem.at[0])
    wait_all(n_dom, recv_ref, send_sem.at[1])


def layer_kernel(
    n_dom, n_feat, hub_dev, per_step, src_ref, source_ref, wide_ref, grad_ref, w_ref,
    out_hbm, gf_ref, back_ref, dw_ref, out_ref, far_acc, out_sem,
):
    blocks, block, reach = wide_ref.shape
    tiles = reach // block
    near = tiles // 2
    nodes, width = gf_ref.shape
    own_blocks = nodes // block
    n = n_dom * n_feat
    slots = back_ref.shape[2] - hub_dev
    halo = slots * n
    gf_ref[...] = jnp.zeros_like(gf_ref)
    far_acc[...] = jnp.zeros_like(far_acc)
    dw_ref[...] = jnp.zeros_like(dw_ref)
    rows = per_step * block

    def flush(step):
        span = pl.ds(pl.multiple_of(step * rows, rows), rows)
        return pltpu.make_async_copy(out_ref.at[span], out_hbm.at[span], out_sem.at[step])

    def body(step, carry):
        summed = []
        for i in range(per_step):
            b = step * per_step + i
            picked = jnp.concatenate(
                [source_ref[pl.ds(pl.multiple_of(src_ref[t, b] * block, block), block)] for t in range(tiles)], 0
            )
            summed.append(jnp.dot(wide_ref[b], picked, preferred_element_type=F32))
        summed = jnp.concatenate(summed, 0)
        inv = 1.0 / (summed[:, width:] + 1.0)
        neighbor = (summed[:, :width] * inv).astype(BF16)
        span = pl.ds(pl.multiple_of(step * rows, rows), rows)
        both = jnp.concatenate([source_ref[span, :width], neighbor], 1)
        preact = jnp.dot(both, w_ref[...], preferred_element_type=F32)
        sigma = 0.5 * jnp.tanh(0.5 * preact) + 0.5
        out = preact * sigma
        out_ref[span] = out.astype(BF16)
        flush(step).start()
        slope = sigma + out * (1.0 - sigma)
        d_pre = (grad_ref[span].astype(F32) * slope).astype(BF16)
        d_both = lax.dot_general(d_pre, w_ref[...], OVER_COLS, preferred_element_type=F32)
        d_neigh = (d_both[:, width:] * inv).astype(BF16)
        gf_ref[span] += d_both[:, :width]
        dw = lax.dot_general(both, d_pre, OVER_ROWS, preferred_element_type=F32)
        dw_ref[0] += dw[:, :width]
        dw_ref[1] += dw[:, width:]
        for i in range(per_step):
            b = step * per_step + i
            pieces = lax.dot_general(
                wide_ref[b], d_neigh[i * block : (i + 1) * block], OVER_ROWS, preferred_element_type=F32
            )
            for t in range(tiles):
                piece = pieces[t * block : (t + 1) * block]
                if t < near:
                    at = pl.ds(pl.multiple_of(src_ref[t, b] * block, block), block)
                    gf_ref[at] += piece
                else:
                    at = pl.ds(pl.multiple_of((src_ref[t, b] - own_blocks) * block, block), block)
                    far_acc[at] += piece
        return carry

    lax.fori_loop(0, blocks // per_step, body, 0)
    for p in range(n):
        d_halo = far_acc[p * slots : (p + 1) * slots]
        back_ref[p % n_feat, p // n_feat, :slots] = d_halo.astype(BF16).astype(F32)
        back_ref[p % n_feat, p // n_feat, slots:] = far_acc[halo + p * hub_dev : halo + (p + 1) * hub_dev]
    for step in range(blocks // per_step):
        flush(step).wait()


def collect_kernel(
    n_dom, n_feat, send_rows, hub_rows, back_ref, dw_ref, gf_ref, out_gf, out_ws, out_wn,
    hop_ref, recv_ref, stage_ref, part_ref, mid_ref, thin_ref, small_ref, line_ref, full_ref, send_sem, recv_sem,
):
    n = n_dom * n_feat
    dom, feat = lax.axis_index("dom"), lax.axis_index("feat")
    barrier = greet(n_dom, n_feat)
    hop_ref[feat] = back_ref[feat]
    part_ref[feat] = dw_ref[feat]
    pl.semaphore_wait(barrier, n_feat + n_dom - 2)
    along = lambda q: (dom, q)
    across = lambda q: (q, feat)
    send_all(n_feat, feat, along, lambda q: back_ref.at[q], hop_ref, send_sem.at[1], recv_sem.at[1])
    send_all(n_feat, feat, along, lambda q: dw_ref.at[q], part_ref, send_sem.at[0], recv_sem.at[0])
    wait_all(n_feat, hop_ref, recv_sem.at[1])
    recv_ref[dom] = hop_ref[:, dom]
    send_all(n_dom, dom, across, lambda q: hop_ref.at[:, q], recv_ref, send_sem.at[5], recv_sem.at[5])
    wait_all(n_feat, part_ref, recv_sem.at[0])
    mid_ref[...] = jnp.sum(part_ref[...], axis=0).reshape(mid_ref.shape)
    thin_ref[dom] = mid_ref[dom]
    send_all(n_dom, dom, across, lambda q: mid_ref.at[q], thin_ref, send_sem.at[2], recv_sem.at[2])

    wait_all(n_dom, recv_ref, recv_sem.at[5])
    slots = back_ref.shape[2] - hub_rows.shape[1]
    width = back_ref.shape[3]
    nodes = gf_ref.shape[0]
    for p in range(n):
        stage_ref[p * slots : (p + 1) * slots] = recv_ref[p // n_feat, p % n_feat, :slots]
    terms = stage_ref[...].astype(BF16)
    hub_sum = jnp.sum(recv_ref[...].reshape(n, -1, width), axis=0)[slots:]
    hub_high = hub_sum.astype(BF16)
    rest = hub_sum - hub_high.astype(F32)
    hub_mid = rest.astype(BF16)
    hub_low = (rest - hub_mid.astype(F32)).astype(BF16)
    hub_terms = jnp.concatenate([hub_high, hub_mid, hub_low], 1)
    part = nodes // 4

    def scatter(c):
        span = pl.ds(c * part, part)
        added = jnp.dot(one_hot_rows(send_rows, c * part, part), terms, preferred_element_type=F32)
        hubs = jnp.dot(one_hot_rows(hub_rows, c * part, part), hub_terms, preferred_element_type=F32)
        hubs = (hubs[:, :width] + hubs[:, width : 2 * width]) + hubs[:, 2 * width :]
        out_gf[span] = gf_ref[span] + (added + hubs)

    scatter(0)
    wait_all(n_dom, thin_ref, recv_sem.at[2])
    small_ref[...] = jnp.sum(thin_ref[...], axis=0).astype(small_ref.dtype)
    line_ref[dom] = small_ref[...]
    send_all(n_dom, dom, across, lambda q: small_ref, line_ref, send_sem.at[3], recv_sem.at[3])
    scatter(1)
    wait_all(n_dom, line_ref, recv_sem.at[3])
    full_ref[feat] = line_ref[...]
    send_all(n_feat, feat, along, lambda q: line_ref, full_ref, send_sem.at[4], recv_sem.at[4])
    scatter(2)
    scatter(3)
    wait_all(n_feat, full_ref, recv_sem.at[4])
    full = full_ref[...].astype(F32).reshape(2, 2, out_ws.shape[0], width)
    for h in range(2):
        out_ws[:, h * width : (h + 1) * width] = full[h, 0]
        out_wn[:, h * width : (h + 1) * width] = full[h, 1]
    wait_all(n_feat, dw_ref, send_sem.at[0])
    wait_all(n_feat, back_ref, send_sem.at[1])
    wait_all(n_dom, recv_ref, send_sem.at[5])
    wait_all(n_dom, mid_ref, send_sem.at[2])
    wait_all(n_dom, line_ref, send_sem.at[3])
    wait_all(n_feat, full_ref, send_sem.at[4])


def per_device(features, grad_out, w_self, w_neigh, tile_src, tile_vals, send_rows, hub_rows):
    n_dom = lax.axis_size("dom")
    n_feat = lax.axis_size("feat")
    n = n_dom * n_feat
    nodes, width = features.shape
    hidden = w_self.shape[1]
    blocks, tiles = tile_src.shape
    block = tile_vals.shape[1]
    hub_dev = hub_rows.shape[1]
    halo = send_rows.shape[1]
    group = halo // n + hub_dev
    far = n * group
    sems = pltpu.SemaphoreType.DMA
    shape = jax.ShapeDtypeStruct
    anywhere = pl.BlockSpec(memory_space=pl.ANY)
    scalars = pl.BlockSpec(memory_space=pltpu.SMEM)
    per_step = 4
    steps = blocks // per_step
    limit = 32 << 20

    source, wide, grad, w_both = pl.pallas_call(
        functools.partial(spread_kernel, n_dom, n_feat, per_step),
        out_shape=[
            shape((nodes + far, 2 * width), BF16),
            shape((blocks, block, tiles * block), BF16),
            shape((nodes, hidden), BF16),
            shape((2 * width, hidden), BF16),
        ],
        in_specs=[VMEM, VMEM] + [anywhere] * 5,
        out_specs=[VMEM] * 4,
        scratch_shapes=[
            pltpu.VMEM((nodes, width), BF16),
            pltpu.VMEM((steps, per_step * tiles, block, block), jnp.int32),
            pltpu.VMEM((far, width), F32),
            pltpu.VMEM((n_feat, n_dom, group, width), F32),
            pltpu.VMEM((n_feat, n_dom, group, width), F32),
            pltpu.VMEM((n_dom, n_feat, group, width), F32),
            sems((4,)),
            sems((steps,)),
            sems((2,)),
            sems((2,)),
        ],
        compiler_params=pltpu.CompilerParams(
            collective_id=0, has_side_effects=True, vmem_limit_bytes=47 << 20
        ),
        name="spread_rows",
    )(
        send_rows, hub_rows, features, grad_out, w_self, w_neigh,
        tile_vals.reshape(steps, per_step * tiles, block, block),
    )

    output, grad_near, back, dw = pl.pallas_call(
        functools.partial(layer_kernel, n_dom, n_feat, hub_dev, per_step),
        out_shape=[
            shape((nodes, hidden), BF16),
            shape((nodes, width), F32),
            shape((n_feat, n_dom, group, width), F32),
            shape((2, 2 * width, width), F32),
        ],
        in_specs=[scalars] + [VMEM] * 4,
        out_specs=[anywhere] + [VMEM] * 3,
        scratch_shapes=[
            pltpu.VMEM((nodes, hidden), BF16),
            pltpu.VMEM((far, width), F32),
            sems((steps,)),
        ],
        compiler_params=pltpu.CompilerParams(vmem_limit_bytes=limit),
        name="layer_both_ways",
    )(tile_src.T, source, wide, grad, w_both)

    chunk = 4 * width // n_feat
    piece = chunk // n_dom
    held = BF16 if piece % 16 == 0 else F32
    grad_feat, grad_ws, grad_wn = pl.pallas_call(
        functools.partial(collect_kernel, n_dom, n_feat),
        out_shape=[shape((nodes, width), F32), shape((width, hidden), F32), shape((width, hidden), F32)],
        in_specs=[VMEM] * 5,
        out_specs=[VMEM] * 3,
        scratch_shapes=[
            pltpu.VMEM((n_feat, n_dom, group, width), F32),
            pltpu.VMEM((n_dom, n_feat, group, width), F32),
            pltpu.VMEM((halo, width), F32),
            pltpu.VMEM((n_feat, chunk, width), F32),
            pltpu.VMEM((n_dom, piece, width), F32),
            pltpu.VMEM((n_dom, piece, width), F32),
            pltpu.VMEM((piece, width), held),
            pltpu.VMEM((n_dom, piece, width), held),
            pltpu.VMEM((n_feat, n_dom, piece, width), held),
            sems((6,)),
            sems((6,)),
        ],
        compiler_params=pltpu.CompilerParams(
            collective_id=1, has_side_effects=True, vmem_limit_bytes=limit
        ),
        name="collect_gradients",
    )(send_rows, hub_rows, back, dw.reshape(n_feat, chunk, width), grad_near)
    return output, grad_feat, grad_ws, grad_wn


def solution(mesh):
    nodes = P(("dom", "feat"), None)
    return jax.shard_map(
        per_device,
        mesh=mesh,
        in_specs=(nodes, nodes, P(), P(), nodes, P(("dom", "feat"), None, None), nodes, nodes),
        out_specs=(nodes, nodes, P(), P()),
        check_vma=False,
    )
```

```python
import functools

import jax
import jax.numpy as jnp
from jax import lax
from jax.experimental import pallas as pl
from jax.experimental.pallas import tpu as pltpu
from jax.sharding import PartitionSpec as P

MESH = pl.DeviceIdType.MESH
F32 = jnp.float32
BF16 = jnp.bfloat16
VMEM = pl.BlockSpec(memory_space=pltpu.VMEM)


def my_place(n_feat):
    return lax.axis_index("dom") * n_feat + lax.axis_index("feat")


def place_id(q, n_feat):
    return (q // n_feat, lax.rem(q, n_feat))


def greet(n, n_feat):
    me = my_place(n_feat)
    barrier = pltpu.get_barrier_semaphore()

    def signal(d, carry):
        peer = lax.rem(me + d, n)
        pl.semaphore_signal(barrier, inc=1, device_id=place_id(peer, n_feat), device_id_type=MESH)
        return carry

    lax.fori_loop(1, n, signal, 0)
    return barrier


def send_all(count, me, place_of, source_of, dest, send_sem, recv_sem):
    def start(d, carry):
        peer = lax.rem(me + d, count)
        pltpu.make_async_remote_copy(
            src_ref=source_of(peer),
            dst_ref=dest.at[me],
            send_sem=send_sem,
            recv_sem=recv_sem,
            device_id=place_of(peer),
            device_id_type=MESH,
        ).start()
        return carry

    lax.fori_loop(1, count, start, 0)


def wait_all(count, ref, sem):
    part = ref.at[pl.ds(0, count - 1)]
    pltpu.make_async_copy(part, part, sem).wait()


def one_hot_rows(ids_ref, first, count):
    at = lax.broadcasted_iota(jnp.int32, (count, ids_ref.shape[1]), 0) + first
    return jnp.where(at == ids_ref[...], 1.0, 0.0).astype(BF16)


OVER_ROWS = (((0,), (0,)), ((), ()))
OVER_COLS = (((1,), (1,)), ((), ()))


def spread_kernel(
    n, n_feat, per_step, send_rows, hub_rows, feat_hbm, grad_hbm, ws_hbm, wn_hbm, vals_hbm,
    source_ref, wide_ref, grad_ref, w_ref,
    feat_ref, vals_ref, stage_ref, send_ref, recv_ref, load_sem, vals_sem, send_sem, recv_sem,
):
    nodes, width = feat_ref.shape
    steps, group, block, _ = vals_ref.shape
    tiles = group // per_step
    halo, hub_dev = send_rows.shape[1], hub_rows.shape[1]
    slots = halo // n
    load_feat = pltpu.make_async_copy(feat_hbm, feat_ref, load_sem.at[0])
    load_feat.start()

    def load_vals(c):
        return pltpu.make_async_copy(vals_hbm.at[c], vals_ref.at[c], vals_sem.at[c])

    for c in range(steps):
        load_vals(c).start()
    loads = [
        pltpu.make_async_copy(grad_hbm, grad_ref, load_sem.at[1]),
        pltpu.make_async_copy(ws_hbm, w_ref.at[:width], load_sem.at[2]),
        pltpu.make_async_copy(wn_hbm, w_ref.at[width:], load_sem.at[3]),
    ]
    for load in loads:
        load.start()
    barrier = greet(n, n_feat)
    me = my_place(n_feat)
    load_feat.wait()
    feat = feat_ref[...]
    picked = lax.dot_general(one_hot_rows(send_rows, 0, nodes), feat, OVER_ROWS, preferred_element_type=F32)
    hubs = lax.dot_general(one_hot_rows(hub_rows, 0, nodes), feat, OVER_ROWS, preferred_element_type=F32)
    for p in range(n):
        send_ref[p, :slots] = picked[p * slots : (p + 1) * slots]
        send_ref[p, slots:] = hubs
    recv_ref[me] = send_ref[me]
    pl.semaphore_wait(barrier, n - 1)
    send_all(n, me, lambda q: place_id(q, n_feat), lambda q: send_ref.at[q], recv_ref, send_sem, recv_sem)
    source_ref[:nodes, :width] = feat
    source_ref[:, width:] = jnp.ones((source_ref.shape[0], width), BF16)

    def convert(c, carry):
        load_vals(c).wait()
        for i in range(per_step):
            b = c * per_step + i
            wide_ref[b] = jnp.concatenate(
                [vals_ref[c, i * tiles + t].astype(F32).astype(BF16) for t in range(tiles)], 1
            )
        return carry

    lax.fori_loop(0, steps, convert, 0)
    for load in loads:
        load.wait()
    wait_all(n, recv_ref, recv_sem)
    for p in range(n):
        stage_ref[p * slots : (p + 1) * slots] = recv_ref[p, :slots]
        stage_ref[halo + p * hub_dev : halo + (p + 1) * hub_dev] = recv_ref[p, slots:]
    source_ref[nodes:, :width] = stage_ref[...].astype(BF16)
    wait_all(n, send_ref, send_sem)


def layer_kernel(
    n, hub_dev, per_step, src_ref, source_ref, wide_ref, grad_ref, w_ref,
    out_hbm, gf_ref, back_ref, dw_ref, out_ref, far_acc, out_sem,
):
    blocks, block, reach = wide_ref.shape
    tiles = reach // block
    near = tiles // 2
    nodes, width = gf_ref.shape
    own_blocks = nodes // block
    slots = back_ref.shape[1] - hub_dev
    halo = slots * n
    gf_ref[...] = jnp.zeros_like(gf_ref)
    far_acc[...] = jnp.zeros_like(far_acc)
    dw_ref[...] = jnp.zeros_like(dw_ref)
    rows = per_step * block

    def flush(step):
        span = pl.ds(pl.multiple_of(step * rows, rows), rows)
        return pltpu.make_async_copy(out_ref.at[span], out_hbm.at[span], out_sem.at[step])

    def body(step, carry):
        summed = []
        for i in range(per_step):
            b = step * per_step + i
            picked = jnp.concatenate(
                [source_ref[pl.ds(pl.multiple_of(src_ref[t, b] * block, block), block)] for t in range(tiles)], 0
            )
            summed.append(jnp.dot(wide_ref[b], picked, preferred_element_type=F32))
        summed = jnp.concatenate(summed, 0)
        inv = 1.0 / (summed[:, width:] + 1.0)
        neighbor = (summed[:, :width] * inv).astype(BF16)
        span = pl.ds(pl.multiple_of(step * rows, rows), rows)
        both = jnp.concatenate([source_ref[span, :width], neighbor], 1)
        preact = jnp.dot(both, w_ref[...], preferred_element_type=F32)
        sigma = 0.5 * jnp.tanh(0.5 * preact) + 0.5
        out = preact * sigma
        out_ref[span] = out.astype(BF16)
        flush(step).start()
        slope = sigma + out * (1.0 - sigma)
        d_pre = (grad_ref[span].astype(F32) * slope).astype(BF16)
        d_both = lax.dot_general(d_pre, w_ref[...], OVER_COLS, preferred_element_type=F32)
        d_neigh = (d_both[:, width:] * inv).astype(BF16)
        gf_ref[span] += d_both[:, :width]
        dw = lax.dot_general(both, d_pre, OVER_ROWS, preferred_element_type=F32)
        dw_ref[0] += dw[:, :width]
        dw_ref[1] += dw[:, width:]
        for i in range(per_step):
            b = step * per_step + i
            pieces = lax.dot_general(
                wide_ref[b], d_neigh[i * block : (i + 1) * block], OVER_ROWS, preferred_element_type=F32
            )
            for t in range(tiles):
                piece = pieces[t * block : (t + 1) * block]
                if t < near:
                    at = pl.ds(pl.multiple_of(src_ref[t, b] * block, block), block)
                    gf_ref[at] += piece
                else:
                    at = pl.ds(pl.multiple_of((src_ref[t, b] - own_blocks) * block, block), block)
                    far_acc[at] += piece
        return carry

    lax.fori_loop(0, blocks // per_step, body, 0)
    for p in range(n):
        d_halo = far_acc[p * slots : (p + 1) * slots]
        back_ref[p, :slots] = d_halo.astype(BF16).astype(F32)
        back_ref[p, slots:] = far_acc[halo + p * hub_dev : halo + (p + 1) * hub_dev]
    for step in range(blocks // per_step):
        flush(step).wait()


def collect_kernel(
    n_dom, n_feat, send_rows, hub_rows, back_ref, dw_ref, gf_ref, out_gf, out_ws, out_wn,
    recv_ref, stage_ref, part_ref, mid_ref, thin_ref, small_ref, line_ref, full_ref, send_sem, recv_sem,
):
    n = n_dom * n_feat
    dom, feat = lax.axis_index("dom"), lax.axis_index("feat")
    barrier = greet(n, n_feat)
    me = my_place(n_feat)
    recv_ref[me] = back_ref[me]
    part_ref[feat] = dw_ref[feat]
    pl.semaphore_wait(barrier, n - 1)
    along = lambda q: (dom, q)
    across = lambda q: (q, feat)
    send_all(n_feat, feat, along, lambda q: dw_ref.at[q], part_ref, send_sem.at[0], recv_sem.at[0])
    wait_all(n_feat, part_ref, recv_sem.at[0])
    mid_ref[...] = jnp.sum(part_ref[...], axis=0).reshape(mid_ref.shape)
    thin_ref[dom] = mid_ref[dom]
    send_all(n_dom, dom, across, lambda q: mid_ref.at[q], thin_ref, send_sem.at[2], recv_sem.at[2])
    send_all(n, me, lambda q: place_id(q, n_feat), lambda q: back_ref.at[q], recv_ref, send_sem.at[1], recv_sem.at[1])

    wait_all(n, recv_ref, recv_sem.at[1])
    slots = back_ref.shape[1] - hub_rows.shape[1]
    width = back_ref.shape[2]
    nodes = gf_ref.shape[0]
    for p in range(n):
        stage_ref[p * slots : (p + 1) * slots] = recv_ref[p, :slots]
    terms = stage_ref[...].astype(BF16)
    hub_sum = jnp.sum(recv_ref[...], axis=0)[slots:]
    hub_high = hub_sum.astype(BF16)
    rest = hub_sum - hub_high.astype(F32)
    hub_mid = rest.astype(BF16)
    hub_low = (rest - hub_mid.astype(F32)).astype(BF16)
    hub_terms = jnp.concatenate([hub_high, hub_mid, hub_low], 1)
    part = nodes // 4

    def scatter(c):
        span = pl.ds(c * part, part)
        added = jnp.dot(one_hot_rows(send_rows, c * part, part), terms, preferred_element_type=F32)
        hubs = jnp.dot(one_hot_rows(hub_rows, c * part, part), hub_terms, preferred_element_type=F32)
        hubs = (hubs[:, :width] + hubs[:, width : 2 * width]) + hubs[:, 2 * width :]
        out_gf[span] = gf_ref[span] + (added + hubs)

    scatter(0)
    wait_all(n_dom, thin_ref, recv_sem.at[2])
    small_ref[...] = jnp.sum(thin_ref[...], axis=0).astype(small_ref.dtype)
    line_ref[dom] = small_ref[...]
    send_all(n_dom, dom, across, lambda q: small_ref, line_ref, send_sem.at[3], recv_sem.at[3])
    scatter(1)
    wait_all(n_dom, line_ref, recv_sem.at[3])
    full_ref[feat] = line_ref[...]
    send_all(n_feat, feat, along, lambda q: line_ref, full_ref, send_sem.at[4], recv_sem.at[4])
    scatter(2)
    scatter(3)
    wait_all(n_feat, full_ref, recv_sem.at[4])
    full = full_ref[...].astype(F32).reshape(2, 2, out_ws.shape[0], width)
    for h in range(2):
        out_ws[:, h * width : (h + 1) * width] = full[h, 0]
        out_wn[:, h * width : (h + 1) * width] = full[h, 1]
    wait_all(n_feat, dw_ref, send_sem.at[0])
    wait_all(n, back_ref, send_sem.at[1])
    wait_all(n_dom, mid_ref, send_sem.at[2])
    wait_all(n_dom, line_ref, send_sem.at[3])
    wait_all(n_feat, full_ref, send_sem.at[4])


def per_device(features, grad_out, w_self, w_neigh, tile_src, tile_vals, send_rows, hub_rows):
    n_dom = lax.axis_size("dom")
    n_feat = lax.axis_size("feat")
    n = n_dom * n_feat
    nodes, width = features.shape
    hidden = w_self.shape[1]
    blocks, tiles = tile_src.shape
    block = tile_vals.shape[1]
    hub_dev = hub_rows.shape[1]
    halo = send_rows.shape[1]
    group = halo // n + hub_dev
    far = n * group
    sems = pltpu.SemaphoreType.DMA
    shape = jax.ShapeDtypeStruct
    anywhere = pl.BlockSpec(memory_space=pl.ANY)
    scalars = pl.BlockSpec(memory_space=pltpu.SMEM)
    per_step = 4
    steps = blocks // per_step
    limit = 32 << 20

    source, wide, grad, w_both = pl.pallas_call(
        functools.partial(spread_kernel, n, n_feat, per_step),
        out_shape=[
            shape((nodes + far, 2 * width), BF16),
            shape((blocks, block, tiles * block), BF16),
            shape((nodes, hidden), BF16),
            shape((2 * width, hidden), BF16),
        ],
        in_specs=[VMEM, VMEM] + [anywhere] * 5,
        out_specs=[VMEM] * 4,
        scratch_shapes=[
            pltpu.VMEM((nodes, width), BF16),
            pltpu.VMEM((steps, per_step * tiles, block, block), jnp.int32),
            pltpu.VMEM((far, width), F32),
            pltpu.VMEM((n, group, width), F32),
            pltpu.VMEM((n, group, width), F32),
            sems((4,)),
            sems((steps,)),
            sems,
            sems,
        ],
        compiler_params=pltpu.CompilerParams(
            collective_id=0, has_side_effects=True, vmem_limit_bytes=47 << 20
        ),
        name="spread_rows",
    )(
        send_rows, hub_rows, features, grad_out, w_self, w_neigh,
        tile_vals.reshape(steps, per_step * tiles, block, block),
    )

    output, grad_near, back, dw = pl.pallas_call(
        functools.partial(layer_kernel, n, hub_dev, per_step),
        out_shape=[
            shape((nodes, hidden), BF16),
            shape((nodes, width), F32),
            shape((n, group, width), F32),
            shape((2, 2 * width, width), F32),
        ],
        in_specs=[scalars] + [VMEM] * 4,
        out_specs=[anywhere] + [VMEM] * 3,
        scratch_shapes=[
            pltpu.VMEM((nodes, hidden), BF16),
            pltpu.VMEM((far, width), F32),
            sems((steps,)),
        ],
        compiler_params=pltpu.CompilerParams(vmem_limit_bytes=limit),
        name="layer_both_ways",
    )(tile_src.T, source, wide, grad, w_both)

    chunk = 4 * width // n_feat
    piece = chunk // n_dom
    held = BF16 if piece % 16 == 0 else F32
    grad_feat, grad_ws, grad_wn = pl.pallas_call(
        functools.partial(collect_kernel, n_dom, n_feat),
        out_shape=[shape((nodes, width), F32), shape((width, hidden), F32), shape((width, hidden), F32)],
        in_specs=[VMEM] * 5,
        out_specs=[VMEM] * 3,
        scratch_shapes=[
            pltpu.VMEM((n, group, width), F32),
            pltpu.VMEM((halo, width), F32),
            pltpu.VMEM((n_feat, chunk, width), F32),
            pltpu.VMEM((n_dom, piece, width), F32),
            pltpu.VMEM((n_dom, piece, width), F32),
            pltpu.VMEM((piece, width), held),
            pltpu.VMEM((n_dom, piece, width), held),
            pltpu.VMEM((n_feat, n_dom, piece, width), held),
            sems((5,)),
            sems((5,)),
        ],
        compiler_params=pltpu.CompilerParams(
            collective_id=1, has_side_effects=True, vmem_limit_bytes=limit
        ),
        name="collect_gradients",
    )(send_rows, hub_rows, back, dw.reshape(n_feat, chunk, width), grad_near)
    return output, grad_feat, grad_ws, grad_wn


def solution(mesh):
    nodes = P(("dom", "feat"), None)
    return jax.shard_map(
        per_device,
        mesh=mesh,
        in_specs=(nodes, nodes, P(), P(), nodes, P(("dom", "feat"), None, None), nodes, nodes),
        out_specs=(nodes, nodes, P(), P()),
        check_vma=False,
    )
```
